32 devices in a mesh: facet: 4 (over x, core), band: 8 (over z, y).
Axes of the slice: x: 2, y: 2, z: 4, core: 2. Of those that a mesh axis runs over, the one named last changes fastest.
Arguments:
- visibilities: bfloat16 [4, 4, 128, 2, 256], P('facet', None, 'band'), may hold values from -6 to 6
- uv_coords: float32 [4, 4, 2, 256], replicated, may hold values from -12 to 12
- aterms: bfloat16 [4, 4, 4, 2, 1024], P('facet'), may hold values from -5 to 5
- offsets: int32 [4, 4, 2, 4], P('facet'), may hold values from 0 to 2016
- counts: int32 [4, 4], P('facet'), may hold values from 1 to 4, as said below
- owner: int32 [4], replicated, may hold values from 0 to 3, as said below
Outputs:
- facet_tiles: float32 [4, 2, 2048, 2048], P('facet', None, 'band')
The draws below stay inside these ranges and needn't reach their ends.
Inputs may be any that keep to these rules, and one draw needn't show every extreme that they name: `owner`: each facet index appears exactly once. `counts`: some entry equals 4.
All inputs are finite; a program needn't handle non-finite values.
Results may differ from the reference program's by a relative error of at most 0.0036.
Values may be sent and summed in bfloat16 or wider, within the bound.
A program may use at most 64 MiB of HBM per device.

```python
import math
import jax
import jax.numpy as jnp
from jax import lax

NPIX = 32
NV = 256
SG = 4
TILE = 2048
BLK_DEV = 1
STEPS = 4
CH = 128
N_FACET = 4


def draw_owner(key, part):
    key = jax.random.fold_in(key, 11)
    shuffled = jax.random.permutation(key, STEPS)
    return (shuffled % (STEPS // BLK_DEV)).astype(jnp.int32)


def draw_counts(key, part):
    key = jax.random.fold_in(key, 23)
    facet_total = STEPS // BLK_DEV
    level_key, step_key = jax.random.split(key)
    facet_level = jax.random.randint(level_key, (facet_total, 1), 1, SG + 1)
    step_level = jax.random.randint(step_key, (facet_total, STEPS), 1, SG + 1)
    live_counts = jnp.maximum(step_level, facet_level)
    live_counts = live_counts.at[0, 0].set(SG)
    return live_counts.astype(jnp.int32)


def set_ends(array, stream_key, least, largest):
    place = [jax.random.randint(jax.random.fold_in(stream_key, axis), (), 0, length) for axis, length in enumerate(array.shape)]
    main_axis = array.shape.index(max(array.shape))
    next_to = place[:main_axis] + [(place[main_axis] + 1) % array.shape[main_axis]] + place[main_axis + 1:]
    return array.at[tuple(place)].set(least).at[tuple(next_to)].set(largest)


def block_scale(stream_key, extent, cuts, low, largest):
    def one(position, parts):
        heights = jax.random.uniform(jax.random.fold_in(jax.random.fold_in(stream_key, 6), position), (parts,), jnp.float32, low / len(cuts), largest / len(cuts))
        return jnp.repeat(jnp.exp(heights), extent[position] // parts).reshape((-1,) + (1,) * (len(extent) - position - 1))

    factor_of = one(*cuts[0])
    for cut in cuts[1:]:
        factor_of = factor_of * one(*cut)
    return factor_of


def normal_values(key, dims, width, bound, cuts=(), kind=jnp.bfloat16):
    values = jax.random.normal(key, dims, jnp.float32) * width
    if len(cuts) > 0:
        values = block_scale(key, dims, cuts, -0.22, 0.18) * values
    return jnp.clip(values, min=-bound, max=bound).astype(kind)


def setup_inputs(seed: int = 0) -> dict:
    streams_of = jax.random.split(jax.random.key(seed), 7)
    visibilities = normal_values(streams_of[0], (STEPS, SG, CH, 2, NV), 1.0, 6.0, ((0, 4), (2, 8)))
    uv_coords = jnp.clip(jax.random.uniform(streams_of[1], (STEPS, SG, 2, NV), jnp.float32, -12.0, 12.0), -12.0, 12.0)
    aterms = normal_values(streams_of[2], (N_FACET, STEPS, SG, 2, NPIX * NPIX), 0.7, 5.0, ((0, 4),))
    offsets = set_ends(jax.random.randint(streams_of[3], (N_FACET, STEPS, 2, SG), 0, TILE - NPIX + 1), jax.random.fold_in(streams_of[3], 1), 0, TILE - NPIX).astype(jnp.int32)
    counts = draw_counts(jax.random.fold_in(streams_of[6], 71), 0)
    owner = draw_owner(jax.random.fold_in(streams_of[6], 71), 0)
    return dict(visibilities=visibilities, uv_coords=uv_coords, aterms=aterms, offsets=offsets, counts=counts, owner=owner)


TWO_PI = 2.0 * math.pi

def dft_tables(side_pix):
    pixel_index = jnp.arange(side_pix, dtype=jnp.int32)
    phase_turns = pixel_index[:, None] * pixel_index[None, :] % side_pix
    dft_angle = TWO_PI * phase_turns.astype(jnp.float32) / side_pix
    return (jnp.cos(dft_angle), jnp.sin(dft_angle))

def subgrid_product(vis_block, coords, chan_freq, pixel_pos, facet_shift):
    u_coord = (coords[0][None, :] * chan_freq[:, None]).reshape(-1)
    v_coord = (coords[1][None, :] * chan_freq[:, None]).reshape(-1)
    vis_real = vis_block[:, 0, :].reshape(-1).astype(jnp.float32)
    vis_imag = vis_block[:, 1, :].reshape(-1).astype(jnp.float32)
    angle_left = TWO_PI * (pixel_pos + facet_shift)[:, None] * u_coord[None, :]
    cos_left = jnp.cos(angle_left)
    sin_left = jnp.sin(angle_left)
    left_ops = jnp.concatenate([cos_left * vis_real - sin_left * vis_imag, sin_left * vis_real + cos_left * vis_imag], axis=0).astype(jnp.bfloat16)
    angle_right = TWO_PI * pixel_pos[:, None] * v_coord[None, :]
    right_ops = jnp.concatenate([jnp.cos(angle_right), jnp.sin(angle_right)], axis=0).astype(jnp.bfloat16)
    left_ops = lax.optimization_barrier(left_ops).astype(jnp.float32)
    right_ops = lax.optimization_barrier(right_ops).astype(jnp.float32)
    return jnp.dot(left_ops, right_ops.T, precision=lax.Precision.HIGHEST)

def image_to_grid(product, aterm_vals, live_weight, dft_cos, dft_sin):
    side_pix = dft_cos.shape[0]
    image_re = product[:side_pix, :side_pix] - product[side_pix:, side_pix:]
    image_im = product[:side_pix, side_pix:] + product[side_pix:, :side_pix]
    gains = aterm_vals.astype(jnp.float32).reshape(2, side_pix, side_pix)
    weighted_re = (image_re * gains[0] - image_im * gains[1]) * live_weight
    weighted_im = (image_re * gains[1] + image_im * gains[0]) * live_weight
    highest = lax.Precision.HIGHEST
    half_re = jnp.dot(dft_cos, weighted_re, precision=highest) + jnp.dot(dft_sin, weighted_im, precision=highest)
    half_im = jnp.dot(dft_cos, weighted_im, precision=highest) - jnp.dot(dft_sin, weighted_re, precision=highest)
    grid_re = jnp.dot(half_re, dft_cos, precision=highest) + jnp.dot(half_im, dft_sin, precision=highest)
    grid_im = jnp.dot(half_im, dft_cos, precision=highest) - jnp.dot(half_re, dft_sin, precision=highest)
    return jnp.stack([grid_re, grid_im])

def add_subgrid(facet_tile, uv_grid, row_start, col_start):
    zero_index = jnp.zeros((), jnp.int32)
    starts = (zero_index, row_start.astype(jnp.int32), col_start.astype(jnp.int32))
    current = lax.dynamic_slice(facet_tile, starts, uv_grid.shape)
    return lax.dynamic_update_slice(facet_tile, current + uv_grid, starts)

def reference(visibilities, uv_coords, aterms, offsets, counts, owner):
    facet_count = aterms.shape[0]
    step_count = owner.shape[0]
    sub_count = uv_coords.shape[1]
    row_count = uv_coords.shape[3]
    chan_total = visibilities.shape[2]
    side_pix = NPIX
    tile_side = TILE
    step_order = jnp.arange(step_count, dtype=jnp.int32)
    same_owner = (owner[None, :] == owner[:, None]) & (step_order[None, :] < step_order[:, None])
    earlier = lax.optimization_barrier(jnp.sum(same_owner.astype(jnp.int32), axis=1)).astype(jnp.int32)
    block_index = (owner * BLK_DEV + earlier).astype(jnp.int32)
    chan_freq = 1.0 + 0.5 * jnp.arange(chan_total, dtype=jnp.int32).astype(jnp.float32) / chan_total
    pixel_pos = (jnp.arange(side_pix, dtype=jnp.int32) - side_pix // 2).astype(jnp.float32) / side_pix
    dft_cos, dft_sin = dft_tables(side_pix)
    norm_scale = 1.0 / (side_pix * math.sqrt(row_count * chan_total))

    def one_facet(facet):
        facet_shift = (facet.astype(jnp.float32) + 0.5) / facet_count - 0.5

        def single_product(vis_sub, coord_sub):
            return subgrid_product(vis_sub, coord_sub, chan_freq, pixel_pos, facet_shift)

        def advance(facet_tile, step_index):
            vis_block = visibilities[block_index[step_index]]
            coords = uv_coords[step_index]
            aterm_step = aterms[facet, step_index]
            place_step = offsets[facet, step_index]
            live_count = counts[facet, step_index]
            products = jax.vmap(single_product)(vis_block, coords)
            for subgrid in range(sub_count):
                live_weight = jnp.where(subgrid < live_count, norm_scale, 0.0).astype(jnp.float32)
                uv_grid = image_to_grid(products[subgrid], aterm_step[subgrid], live_weight, dft_cos, dft_sin)
                facet_tile = add_subgrid(facet_tile, uv_grid, place_step[0, subgrid], place_step[1, subgrid])
            return (facet_tile, None)
        empty_tile = jnp.zeros((2, tile_side, tile_side), jnp.float32)
        facet_tile, unused = lax.scan(advance, empty_tile, step_order)
        return facet_tile
    return lax.map(one_facet, jnp.arange(facet_count, dtype=jnp.int32))
```

```python
import functools
import math

import jax
import jax.numpy as jnp
import numpy as np
from jax import lax
from jax.experimental import pallas as pl
from jax.experimental.pallas import tpu as pltpu
from jax.sharding import PartitionSpec as P

NPIX = 32
TILE = 2048
TWO_PI = 2.0 * math.pi
MESH = pl.DeviceIdType.MESH
HIGHEST = lax.Precision.HIGHEST
ROWS = 64


def cmul(a, b):
    return a[0] * b[0] - a[1] * b[1], a[0] * b[1] + a[1] * b[0]


def cheb(two_cos, now, before):
    return two_cos * now[0] - before[0], two_cos * now[1] - before[1]


def pick(mask, a, b):
    return jnp.where(mask, a[0], b[0]), jnp.where(mask, a[1], b[1])


def image_kernel(
    sizes, owner_ref, uv_ref, vis_ref, ate_ref, dft_ref, sel_ref, out_ref,
    pow_ref, left_ref, right_ref, part_ref, got_ref, sum_ref, gain_ref, send_ref, band_ref,
    send_sem, recv_sem, send2_sem, recv2_sem,
):
    facets, bands, steps, subs, chans, width = sizes
    per_band = NPIX // bands
    lanes = per_band * NPIX
    total = facets * bands
    fac, band = lax.axis_index("facet"), lax.axis_index("band")
    me = fac * bands + band

    barrier = pltpu.get_barrier_semaphore()

    def greet(k, carry):
        to = lax.rem(me + k, total)
        pl.semaphore_signal(
            barrier, inc=1, device_id=(to // bands, lax.rem(to, bands)), device_id_type=MESH
        )
        return carry

    lax.fori_loop(1, total, greet, 0)

    step = jnp.int32(0)
    for t in range(steps):
        step = jnp.where(owner_ref[t] == fac, t, step)
    chan = band * chans + lax.broadcasted_iota(jnp.int32, (chans, 1), 0)
    freq = 1.0 + 0.5 * chan.astype(jnp.float32) / (chans * bands)
    for s in range(subs):
        uv = uv_ref[step, s]
        rows = pl.ds(s * chans, chans)
        for axis in range(2):
            angle = (TWO_PI / NPIX) * (uv[axis : axis + 1, :] * freq)
            w1 = (jnp.cos(angle), jnp.sin(angle))
            w2 = cmul(w1, w1)
            w4 = cmul(w2, w2)
            w8 = cmul(w4, w4)
            if axis == 0:
                w16 = cmul(w8, w8)
                kept = (w1, w4, w8, cmul(w4, w8), w16, cmul(w16, w16))
            else:
                kept = (w1, w2, cmul(w1, w2), w4, w8)
            for i, w in enumerate(kept):
                pow_ref[12 * axis + 2 * i, rows, :] = w[0]
                pow_ref[12 * axis + 2 * i + 1, rows, :] = w[1]

    j = lax.broadcasted_iota(jnp.int32, (8, width), 0)
    bit0, bit1, bit2 = (j & 1) == 1, (j & 2) == 2, (j & 4) == 4
    one = (jnp.ones((8, width), jnp.float32), jnp.zeros((8, width), jnp.float32))

    def subgrid(s):
        for c in range(chans):
            row = pl.ds(s * chans + c, 1)

            def power(index):
                return tuple(
                    jnp.broadcast_to(pow_ref[2 * index + part, row, :], (8, width))
                    for part in range(2)
                )

            cols = pl.ds(c * width, width)
            w1, w4, w8, w12, w16, w32 = (power(i) for i in range(6))
            value = vis_ref[0, s, c].astype(jnp.float32)
            vis = (
                jnp.broadcast_to(value[0:1], (8, width)),
                jnp.broadcast_to(value[1:2], (8, width)),
            )
            e = pick(bit1, pick(bit0, w12, w8), pick(bit0, w4, one))
            e = cmul(e, pick(bit2, w16, one))
            upper = cmul(vis, e)
            lower = cmul(upper, (w32[0], -w32[1]))
            two_cos = 2.0 * w1[0]
            seq_u = [upper, cmul(upper, w1)]
            seq_l = [lower, cmul(lower, w1)]
            for i in range(2, 4):
                seq_u.append(cheb(two_cos, seq_u[i - 1], seq_u[i - 2]))
                seq_l.append(cheb(two_cos, seq_l[i - 1], seq_l[i - 2]))
            for i in range(4):
                for part in range(2):
                    left_ref[pl.ds(ROWS * part + 16 * i, 16), cols] = jnp.concatenate(
                        [seq_l[i][part], seq_u[i][part]], axis=0
                    ).astype(jnp.bfloat16)
            r1, r2, r3, r4, r8 = (power(6 + i) for i in range(5))
            e = pick(bit1, pick(bit0, r3, r2), pick(bit0, r1, one))
            m2 = cmul(e, pick(bit2, r4, one))
            m3 = cmul(m2, r8)
            two_cos = 2.0 * r8[0]
            m1 = cheb(two_cos, m2, m3)
            m0 = cheb(two_cos, m1, m2)
            for part in range(2):
                right_ref[pl.ds(NPIX * part, 16), cols] = jnp.concatenate(
                    [m0[part], m1[part]], axis=0
                ).astype(jnp.bfloat16)
                right_ref[pl.ds(NPIX * part + 16, 16), cols] = jnp.concatenate(
                    [m2[part], m3[part]], axis=0
                ).astype(jnp.bfloat16)
        prod = lax.dot_general(
            left_ref[...], right_ref[...], (((1,), (1,)), ((), ())),
            preferred_element_type=jnp.float32,
        )
        re = prod[:ROWS, :NPIX] - prod[ROWS:, NPIX:]
        im = prod[:ROWS, NPIX:] + prod[ROWS:, :NPIX]
        for part, image in enumerate((re, im)):
            for high in range(4 // per_band):
                pieces = [
                    image[16 * (high * per_band + i) : 16 * (high * per_band + i) + 16]
                    for i in range(per_band)
                ]
                part_ref[:, high, 2 * s + part, :] = jnp.concatenate(pieces, axis=1)

    for s in range(subs):
        subgrid(s)

    pl.semaphore_wait(barrier, total - 1)

    groups = 4 // per_band

    def source(to):
        at = (to // bands * (NPIX // facets) + NPIX // 2 // facets) // per_band + lax.rem(to, bands)
        return part_ref.at[at // groups, lax.rem(at, groups)]

    def spread(k, carry):
        to = lax.rem(me + k, total)
        pltpu.make_async_remote_copy(
            src_ref=source(to), dst_ref=got_ref.at[k], send_sem=send_sem, recv_sem=recv_sem,
            device_id=(to // bands, lax.rem(to, bands)), device_id_type=MESH,
        ).start()
        return carry

    lax.fori_loop(1, total, spread, 0)
    got_ref[0] = source(me)[...]

    first = band * lanes // 128
    chunk = pl.ds(pl.multiple_of(first * 128, 128), 128)
    for t in range(steps):
        for s in range(subs):
            gain = ate_ref[0, t, s, :, chunk].astype(jnp.float32)
            if lanes < 128:
                shift = lax.rem(band * lanes, 128)
                gain = sum(
                    jnp.where(shift == at, gain[:, at : at + lanes], 0.0)
                    for at in range(0, 128, lanes)
                )
            gain_ref[pl.ds(8 * t + 2 * s, 2), :] = gain

    def wait_all(buf, count, sem):
        view = buf.at[pl.ds(1, count)]
        pltpu.make_async_copy(view, view, sem).wait()

    wait_all(got_ref, total - 1, recv_sem)
    for g in range(facets):
        acc = got_ref[lax.rem(me - g * bands + total, total)]
        for b in range(1, bands):
            acc = acc + got_ref[lax.rem(me - g * bands - b + 2 * total, total)]
        sum_ref[g] = acc
    image = jnp.concatenate([sum_ref[owner_ref[t]] for t in range(steps)], axis=0)
    gains = gain_ref[...]
    count = 8 * steps
    even = lax.broadcasted_iota(jnp.int32, (count, lanes), 0) % 2 == 0

    def nxt(x):
        return jnp.concatenate([x[1:], x[:1]], axis=0)

    def prev(x):
        return jnp.concatenate([x[-1:], x[:-1]], axis=0)

    straight = image * gains
    crossed = image * jnp.where(even, nxt(gains), prev(gains))
    weighted = jnp.where(even, straight - nxt(straight), crossed + prev(crossed))
    turned = jnp.where(even, nxt(weighted), -prev(weighted))
    both = jnp.concatenate([weighted, turned], axis=1)
    pixel = lax.broadcasted_iota(jnp.int32, both.shape, 1) % lanes // NPIX
    stacked = jnp.concatenate([jnp.where(pixel == i, both, 0.0) for i in range(per_band)], axis=0)
    half = jnp.dot(stacked, dft_ref[...], precision=HIGHEST, preferred_element_type=jnp.float32)
    row_sub = lax.broadcasted_iota(jnp.int32, half.shape, 0) % 8 // 2
    lane_sub = lax.broadcasted_iota(jnp.int32, half.shape, 1) // NPIX
    half = jnp.where(row_sub == lane_sub, half, 0.0)
    half = jnp.dot(sel_ref[...], half, precision=HIGHEST, preferred_element_type=jnp.float32)
    send_ref[...] = half.astype(jnp.bfloat16)

    def share(k, carry):
        pltpu.make_async_remote_copy(
            src_ref=send_ref, dst_ref=band_ref.at[k], send_sem=send2_sem, recv_sem=recv2_sem,
            device_id=(fac, lax.rem(band + k, bands)), device_id_type=MESH,
        ).start()
        return carry

    lax.fori_loop(1, bands, share, 0)
    band_ref[0] = send_ref[...]
    wait_all(band_ref, bands - 1, recv2_sem)
    group = 2 * per_band
    for b in range(bands):
        block = band_ref[lax.rem(band - b + bands, bands)].astype(jnp.float32)
        for t in range(steps):
            out_ref[t, pl.ds(group * b, group), :] = block[group * t : group * t + group]
    wait_all(got_ref, total - 1, send_sem)
    wait_all(band_ref, bands - 1, send2_sem)


def place_kernel(sizes, scale, off_ref, cnt_ref, half_ref, dft_ref, out_ref, grid_ref, tile_ref, sem):
    steps, subs, rows, cols = sizes
    base = lax.axis_index("band") * rows
    tile_ref[:, pl.ds(NPIX, rows), :] = jnp.zeros((2, rows, cols), jnp.float32)
    lane = lax.broadcasted_iota(jnp.int32, (2 * NPIX, 128), 1)

    def one_step(t, carry):
        grid_ref[...] = scale * jnp.dot(
            dft_ref[...], half_ref[t], precision=HIGHEST, preferred_element_type=jnp.float32
        )
        for s in range(subs):
            row = off_ref[0, t, 0, s] - base
            col = off_ref[0, t, 1, s]
            live = (s < cnt_ref[0, t]) & (row > -NPIX) & (row < rows)

            @pl.when(live)
            def _():
                shift = col % 128
                left = pl.multiple_of(col - shift, 128)
                grid = jnp.where(lane // NPIX == s, grid_ref[...], 0.0)
                grid = pltpu.roll(grid, (shift + 128 - NPIX * s) % 128, 1)
                down = (row + NPIX) % 8
                top = pl.multiple_of(row + NPIX - down, 8)
                tail = jnp.zeros((8, 128), jnp.float32)
                parts = [
                    pltpu.roll(
                        jnp.concatenate([grid[NPIX * part : NPIX * part + NPIX], tail], axis=0),
                        down, 0,
                    )
                    for part in range(2)
                ]
                span = lane[: NPIX + 8]
                for part in range(2):
                    spot = (part, pl.ds(top, NPIX + 8), pl.ds(left, 128))
                    tile_ref[spot] += jnp.where(span >= shift, parts[part], 0.0)

                @pl.when(shift > 128 - NPIX)
                def _():
                    right = pl.multiple_of(left + 128, 128)
                    for part in range(2):
                        spot = (part, pl.ds(top, NPIX + 8), pl.ds(right, 128))
                        tile_ref[spot] += jnp.where(span < shift, parts[part], 0.0)

        return carry

    lax.fori_loop(0, steps, one_step, 0)
    copy = pltpu.make_async_copy(tile_ref.at[:, pl.ds(NPIX, rows), :], out_ref.at[0], sem)
    copy.start()
    copy.wait()


def tables(bands, steps, subs):
    per_band = NPIX // bands
    k = np.arange(NPIX)
    angle = 2.0 * np.pi * (k[:, None] * k[None, :] % NPIX) / NPIX
    cos, sin = np.cos(angle), np.sin(angle)
    lanes_dft = np.concatenate(
        [np.tile(cos, (per_band, subs)), np.tile(sin, (per_band, subs))], axis=0
    )
    select = np.zeros((steps, 2, per_band, per_band, steps, subs, 2))
    for t in range(steps):
        for part in range(2):
            for i in range(per_band):
                select[t, part, i, i, t, :, part] = 1.0
    select = select.reshape(steps * 2 * per_band, per_band * steps * subs * 2)
    blocks = np.stack([np.stack([cos, sin]), np.stack([-sin, cos])])
    rows_dft = blocks.reshape(2, 2, NPIX, bands, per_band).transpose(0, 2, 3, 1, 4)
    rows_dft = rows_dft.reshape(2 * NPIX, 2 * NPIX)
    return [np.asarray(x, np.float32) for x in (lanes_dft, select, rows_dft)]


def body(visibilities, uv_coords, aterms, offsets, counts, owner):
    facets, bands = lax.axis_size("facet"), lax.axis_size("band")
    subs, chans, width = visibilities.shape[1], visibilities.shape[2], visibilities.shape[4]
    steps = owner.shape[0]
    per_band = NPIX // bands
    lanes = per_band * NPIX
    total = facets * bands
    lanes_dft, select, rows_dft = tables(bands, steps, subs)
    vmem = pl.BlockSpec(memory_space=pltpu.VMEM)
    smem = pl.BlockSpec(memory_space=pltpu.SMEM)
    f32, bf16 = jnp.float32, jnp.bfloat16
    dma = pltpu.SemaphoreType.DMA(())
    half = pl.pallas_call(
        functools.partial(image_kernel, (facets, bands, steps, subs, chans, width)),
        out_shape=jax.ShapeDtypeStruct((steps, 2 * NPIX, subs * NPIX), f32),
        in_specs=[smem] + [vmem] * 5,
        out_specs=vmem,
        scratch_shapes=[
            pltpu.VMEM((22, subs * chans, width), f32),
            pltpu.VMEM((2 * ROWS, chans * width), bf16),
            pltpu.VMEM((2 * NPIX, chans * width), bf16),
            pltpu.VMEM((16, 4 // per_band, 2 * subs, lanes), f32),
            pltpu.VMEM((total, 2 * subs, lanes), f32),
            pltpu.VMEM((facets, 2 * subs, lanes), f32),
            pltpu.VMEM((8 * steps, lanes), f32),
            pltpu.VMEM((2 * steps * per_band, subs * NPIX), bf16),
            pltpu.VMEM((bands, 2 * steps * per_band, subs * NPIX), bf16),
            dma, dma, dma, dma,
        ],
        compiler_params=pltpu.CompilerParams(
            collective_id=0, has_side_effects=True, vmem_limit_bytes=32 * 1024 * 1024
        ),
    )(owner, uv_coords, visibilities, aterms, lanes_dft, select)
    rows = TILE // bands
    scale = 1.0 / (NPIX * math.sqrt(width * chans * bands))
    return pl.pallas_call(
        functools.partial(place_kernel, (steps, subs, rows, TILE), scale),
        out_shape=jax.ShapeDtypeStruct((1, 2, rows, TILE), f32),
        in_specs=[smem, smem, vmem, vmem],
        out_specs=pl.BlockSpec(memory_space=pl.ANY),
        scratch_shapes=[
            pltpu.VMEM((2 * NPIX, subs * NPIX), f32),
            pltpu.VMEM((2, rows + 2 * NPIX, TILE), f32),
            dma,
        ],
        compiler_params=pltpu.CompilerParams(vmem_limit_bytes=32 * 1024 * 1024),
    )(offsets, counts, half, rows_dft)


def solution(mesh):
    placed = (
        P("facet", None, "band", None, None),
        P(),
        P("facet", None, None, None, None),
        P("facet", None, None, None),
        P("facet", None),
        P(),
    )
    return jax.shard_map(
        body, mesh=mesh, in_specs=placed, out_specs=P("facet", None, "band", None), check_vma=False
    )
```

```python
import functools
import math

import jax
import jax.numpy as jnp
import numpy as np
from jax import lax
from jax.experimental import pallas as pl
from jax.experimental.pallas import tpu as pltpu
from jax.sharding import PartitionSpec as P

NPIX = 32
TILE = 2048
TWO_PI = 2.0 * math.pi
MESH = pl.DeviceIdType.MESH
HIGHEST = lax.Precision.HIGHEST
VMEM_LIMIT = 60 * 1024 * 1024
ROWS = 64


def cmul(a, b):
    return a[0] * b[0] - a[1] * b[1], a[0] * b[1] + a[1] * b[0]


def cheb(two_cos, now, before):
    return two_cos * now[0] - before[0], two_cos * now[1] - before[1]


def pick(mask, a, b):
    return jnp.where(mask, a[0], b[0]), jnp.where(mask, a[1], b[1])


def image_kernel(
    sizes, owner_hbm, uv_hbm, vis_hbm, ate_hbm, dft_hbm, sel_hbm, out_ref,
    owner_ref, uv_ref, vis_ref, ate_ref, dft_ref, sel_ref, load_sem,
    pow_ref, left_ref, right_ref, part_ref, got_ref, sum_ref, gain_ref, send_ref, band_ref,
    send_sem, recv_sem, send2_sem, recv2_sem,
):
    facets, bands, steps, subs, chans, width = sizes
    per_band = NPIX // bands
    lanes = per_band * NPIX
    total = facets * bands
    fac, band = lax.axis_index("facet"), lax.axis_index("band")
    me = fac * bands + band

    first = band * lanes // 128
    chunk = pl.ds(pl.multiple_of(first * 128, 128), 128)
    loads = [
        pltpu.make_async_copy(src, dst, load_sem.at[i])
        for i, (src, dst) in enumerate((
            (owner_hbm, owner_ref), (uv_hbm, uv_ref), (vis_hbm.at[0], vis_ref),
            (ate_hbm.at[0, :, :, :, chunk], ate_ref), (dft_hbm, dft_ref), (sel_hbm, sel_ref),
        ))
    ]
    for load in loads:
        load.start()
    barrier = pltpu.get_barrier_semaphore()

    def greet(k, carry):
        to = lax.rem(me + k, total)
        pl.semaphore_signal(
            barrier, inc=1, device_id=(to // bands, lax.rem(to, bands)), device_id_type=MESH
        )
        return carry

    lax.fori_loop(1, total, greet, 0)

    for load in loads[:3]:
        load.wait()
    step = jnp.int32(0)
    for t in range(steps):
        step = jnp.where(owner_ref[t] == fac, t, step)
    chan = band * chans + lax.broadcasted_iota(jnp.int32, (chans, 1), 0)
    freq = 1.0 + 0.5 * chan.astype(jnp.float32) / (chans * bands)
    for s in range(subs):
        uv = uv_ref[step, s]
        rows = pl.ds(s * chans, chans)
        for axis in range(2):
            angle = (TWO_PI / NPIX) * (uv[axis : axis + 1, :] * freq)
            w1 = (jnp.cos(angle), jnp.sin(angle))
            w2 = cmul(w1, w1)
            w4 = cmul(w2, w2)
            w8 = cmul(w4, w4)
            if axis == 0:
                w16 = cmul(w8, w8)
                kept = (w1, w4, w8, cmul(w4, w8), w16, cmul(w16, w16))
            else:
                kept = (w1, w2, cmul(w1, w2), w4, w8)
            for i, w in enumerate(kept):
                pow_ref[12 * axis + 2 * i, rows, :] = w[0]
                pow_ref[12 * axis + 2 * i + 1, rows, :] = w[1]

    j = lax.broadcasted_iota(jnp.int32, (8, width), 0)
    bit0, bit1, bit2 = (j & 1) == 1, (j & 2) == 2, (j & 4) == 4
    one = (jnp.ones((8, width), jnp.float32), jnp.zeros((8, width), jnp.float32))

    def subgrid(s):
        for c in range(chans):
            row = pl.ds(s * chans + c, 1)

            def power(index):
                return tuple(
                    jnp.broadcast_to(pow_ref[2 * index + part, row, :], (8, width))
                    for part in range(2)
                )

            cols = pl.ds(c * width, width)
            w1, w4, w8, w12, w16, w32 = (power(i) for i in range(6))
            value = vis_ref[s, c].astype(jnp.float32)
            vis = (
                jnp.broadcast_to(value[0:1], (8, width)),
                jnp.broadcast_to(value[1:2], (8, width)),
            )
            e = pick(bit1, pick(bit0, w12, w8), pick(bit0, w4, one))
            e = cmul(e, pick(bit2, w16, one))
            upper = cmul(vis, e)
            lower = cmul(upper, (w32[0], -w32[1]))
            two_cos = 2.0 * w1[0]
            seq_u = [upper, cmul(upper, w1)]
            seq_l = [lower, cmul(lower, w1)]
            for i in range(2, 4):
                seq_u.append(cheb(two_cos, seq_u[i - 1], seq_u[i - 2]))
                seq_l.append(cheb(two_cos, seq_l[i - 1], seq_l[i - 2]))
            for i in range(4):
                for part in range(2):
                    left_ref[pl.ds(ROWS * part + 16 * i, 16), cols] = jnp.concatenate(
                        [seq_l[i][part], seq_u[i][part]], axis=0
                    ).astype(jnp.bfloat16)
            r1, r2, r3, r4, r8 = (power(6 + i) for i in range(5))
            e = pick(bit1, pick(bit0, r3, r2), pick(bit0, r1, one))
            m2 = cmul(e, pick(bit2, r4, one))
            m3 = cmul(m2, r8)
            two_cos = 2.0 * r8[0]
            m1 = cheb(two_cos, m2, m3)
            m0 = cheb(two_cos, m1, m2)
            for part in range(2):
                right_ref[pl.ds(NPIX * part, 16), cols] = jnp.concatenate(
                    [m0[part], m1[part]], axis=0
                ).astype(jnp.bfloat16)
                right_ref[pl.ds(NPIX * part + 16, 16), cols] = jnp.concatenate(
                    [m2[part], m3[part]], axis=0
                ).astype(jnp.bfloat16)
        prod = lax.dot_general(
            left_ref[...], right_ref[...], (((1,), (1,)), ((), ())),
            preferred_element_type=jnp.float32,
        )
        re = prod[:ROWS, :NPIX] - prod[ROWS:, NPIX:]
        im = prod[:ROWS, NPIX:] + prod[ROWS:, :NPIX]
        for part, image in enumerate((re, im)):
            for high in range(4 // per_band):
                pieces = [
                    image[16 * (high * per_band + i) : 16 * (high * per_band + i) + 16]
                    for i in range(per_band)
                ]
                part_ref[:, high, 2 * s + part, :] = jnp.concatenate(pieces, axis=1)

    for s in range(subs):
        subgrid(s)

    pl.semaphore_wait(barrier, total - 1)

    groups = 4 // per_band

    def source(to):
        at = (to // bands * (NPIX // facets) + NPIX // 2 // facets) // per_band + lax.rem(to, bands)
        return part_ref.at[at // groups, lax.rem(at, groups)]

    def spread(k, carry):
        to = lax.rem(me + k, total)
        pltpu.make_async_remote_copy(
            src_ref=source(to), dst_ref=got_ref.at[k], send_sem=send_sem, recv_sem=recv_sem,
            device_id=(to // bands, lax.rem(to, bands)), device_id_type=MESH,
        ).start()
        return carry

    lax.fori_loop(1, total, spread, 0)
    got_ref[0] = source(me)[...]

    for load in loads[3:]:
        load.wait()
    for t in range(steps):
        for s in range(subs):
            gain = ate_ref[t, s].astype(jnp.float32)
            if lanes < 128:
                shift = lax.rem(band * lanes, 128)
                gain = sum(
                    jnp.where(shift == at, gain[:, at : at + lanes], 0.0)
                    for at in range(0, 128, lanes)
                )
            gain_ref[pl.ds(8 * t + 2 * s, 2), :] = gain

    def wait_all(buf, count, sem):
        view = buf.at[pl.ds(1, count)]
        pltpu.make_async_copy(view, view, sem).wait()

    wait_all(got_ref, total - 1, recv_sem)
    for g in range(facets):
        acc = got_ref[lax.rem(me - g * bands + total, total)]
        for b in range(1, bands):
            acc = acc + got_ref[lax.rem(me - g * bands - b + 2 * total, total)]
        sum_ref[g] = acc
    image = jnp.concatenate([sum_ref[owner_ref[t]] for t in range(steps)], axis=0)
    gains = gain_ref[...]
    count = 8 * steps
    even = lax.broadcasted_iota(jnp.int32, (count, lanes), 0) % 2 == 0

    def nxt(x):
        return jnp.concatenate([x[1:], x[:1]], axis=0)

    def prev(x):
        return jnp.concatenate([x[-1:], x[:-1]], axis=0)

    straight = image * gains
    crossed = image * jnp.where(even, nxt(gains), prev(gains))
    weighted = jnp.where(even, straight - nxt(straight), crossed + prev(crossed))
    turned = jnp.where(even, nxt(weighted), -prev(weighted))
    both = jnp.concatenate([weighted, turned], axis=1)
    pixel = lax.broadcasted_iota(jnp.int32, both.shape, 1) % lanes // NPIX
    stacked = jnp.concatenate([jnp.where(pixel == i, both, 0.0) for i in range(per_band)], axis=0)
    half = jnp.dot(stacked, dft_ref[...], precision=HIGHEST, preferred_element_type=jnp.float32)
    row_sub = lax.broadcasted_iota(jnp.int32, half.shape, 0) % 8 // 2
    lane_sub = lax.broadcasted_iota(jnp.int32, half.shape, 1) // NPIX
    half = jnp.where(row_sub == lane_sub, half, 0.0)
    half = jnp.dot(sel_ref[...], half, precision=HIGHEST, preferred_element_type=jnp.float32)
    send_ref[...] = half.astype(jnp.bfloat16)

    def share(k, carry):
        pltpu.make_async_remote_copy(
            src_ref=send_ref, dst_ref=band_ref.at[k], send_sem=send2_sem, recv_sem=recv2_sem,
            device_id=(fac, lax.rem(band + k, bands)), device_id_type=MESH,
        ).start()
        return carry

    lax.fori_loop(1, bands, share, 0)
    band_ref[0] = send_ref[...]
    wait_all(band_ref, bands - 1, recv2_sem)
    group = 2 * per_band
    for b in range(bands):
        block = band_ref[lax.rem(band - b + bands, bands)].astype(jnp.float32)
        for t in range(steps):
            out_ref[t, pl.ds(group * b, group), :] = block[group * t : group * t + group]
    wait_all(got_ref, total - 1, send_sem)
    wait_all(band_ref, bands - 1, send2_sem)


def place_kernel(
    sizes, scale, off_hbm, cnt_hbm, half_hbm, dft_hbm, out_ref,
    off_ref, cnt_ref, half_ref, dft_ref, grid_ref, tile_ref, load_sem, sem,
):
    steps, subs, rows, cols = sizes
    loads = [
        pltpu.make_async_copy(src, dst, load_sem.at[i])
        for i, (src, dst) in enumerate((
            (off_hbm, off_ref), (cnt_hbm, cnt_ref), (half_hbm, half_ref), (dft_hbm, dft_ref),
        ))
    ]
    for load in loads:
        load.start()
    base = lax.axis_index("band") * rows
    tile_ref[:, pl.ds(NPIX, rows), :] = jnp.zeros((2, rows, cols), jnp.float32)
    lane = lax.broadcasted_iota(jnp.int32, (2 * NPIX, 128), 1)
    for load in loads:
        load.wait()

    def one_step(t, carry):
        grid_ref[...] = scale * jnp.dot(
            dft_ref[...], half_ref[t], precision=HIGHEST, preferred_element_type=jnp.float32
        )
        for s in range(subs):
            row = off_ref[0, t, 0, s] - base
            col = off_ref[0, t, 1, s]
            live = (s < cnt_ref[0, t]) & (row > -NPIX) & (row < rows)

            @pl.when(live)
            def _():
                shift = col % 128
                left = pl.multiple_of(col - shift, 128)
                grid = jnp.where(lane // NPIX == s, grid_ref[...], 0.0)
                grid = pltpu.roll(grid, (shift + 128 - NPIX * s) % 128, 1)
                down = (row + NPIX) % 8
                top = pl.multiple_of(row + NPIX - down, 8)
                tail = jnp.zeros((8, 128), jnp.float32)
                parts = [
                    pltpu.roll(
                        jnp.concatenate([grid[NPIX * part : NPIX * part + NPIX], tail], axis=0),
                        down, 0,
                    )
                    for part in range(2)
                ]
                span = lane[: NPIX + 8]
                for part in range(2):
                    spot = (part, pl.ds(top, NPIX + 8), pl.ds(left, 128))
                    tile_ref[spot] += jnp.where(span >= shift, parts[part], 0.0)

                @pl.when(shift > 128 - NPIX)
                def _():
                    right = pl.multiple_of(left + 128, 128)
                    for part in range(2):
                        spot = (part, pl.ds(top, NPIX + 8), pl.ds(right, 128))
                        tile_ref[spot] += jnp.where(span < shift, parts[part], 0.0)

        return carry

    lax.fori_loop(0, steps, one_step, 0)
    copy = pltpu.make_async_copy(tile_ref.at[:, pl.ds(NPIX, rows), :], out_ref.at[0], sem)
    copy.start()
    copy.wait()


def tables(bands, steps, subs):
    per_band = NPIX // bands
    k = np.arange(NPIX)
    angle = 2.0 * np.pi * (k[:, None] * k[None, :] % NPIX) / NPIX
    cos, sin = np.cos(angle), np.sin(angle)
    lanes_dft = np.concatenate(
        [np.tile(cos, (per_band, subs)), np.tile(sin, (per_band, subs))], axis=0
    )
    select = np.zeros((steps, 2, per_band, per_band, steps, subs, 2))
    for t in range(steps):
        for part in range(2):
            for i in range(per_band):
                select[t, part, i, i, t, :, part] = 1.0
    select = select.reshape(steps * 2 * per_band, per_band * steps * subs * 2)
    blocks = np.stack([np.stack([cos, sin]), np.stack([-sin, cos])])
    rows_dft = blocks.reshape(2, 2, NPIX, bands, per_band).transpose(0, 2, 3, 1, 4)
    rows_dft = rows_dft.reshape(2 * NPIX, 2 * NPIX)
    return [np.asarray(x, np.float32) for x in (lanes_dft, select, rows_dft)]


def body(visibilities, uv_coords, aterms, offsets, counts, owner):
    facets, bands = lax.axis_size("facet"), lax.axis_size("band")
    subs, chans, width = visibilities.shape[1], visibilities.shape[2], visibilities.shape[4]
    steps = owner.shape[0]
    per_band = NPIX // bands
    lanes = per_band * NPIX
    total = facets * bands
    lanes_dft, select, rows_dft = tables(bands, steps, subs)
    vmem = pl.BlockSpec(memory_space=pltpu.VMEM)
    hbm = pl.BlockSpec(memory_space=pltpu.HBM)
    f32, bf16 = jnp.float32, jnp.bfloat16
    dma = pltpu.SemaphoreType.DMA(())
    half = pl.pallas_call(
        functools.partial(image_kernel, (facets, bands, steps, subs, chans, width)),
        out_shape=jax.ShapeDtypeStruct((steps, 2 * NPIX, subs * NPIX), f32),
        in_specs=[hbm] * 6,
        out_specs=vmem,
        scratch_shapes=[
            pltpu.SMEM(owner.shape, jnp.int32),
            pltpu.VMEM(uv_coords.shape, f32),
            pltpu.VMEM(visibilities.shape[1:], bf16),
            pltpu.VMEM((steps, subs, 2, 128), bf16),
            pltpu.VMEM(lanes_dft.shape, f32),
            pltpu.VMEM(select.shape, f32),
            pltpu.SemaphoreType.DMA((6,)),
            pltpu.VMEM((22, subs * chans, width), f32),
            pltpu.VMEM((2 * ROWS, chans * width), bf16),
            pltpu.VMEM((2 * NPIX, chans * width), bf16),
            pltpu.VMEM((16, 4 // per_band, 2 * subs, lanes), f32),
            pltpu.VMEM((total, 2 * subs, lanes), f32),
            pltpu.VMEM((facets, 2 * subs, lanes), f32),
            pltpu.VMEM((8 * steps, lanes), f32),
            pltpu.VMEM((2 * steps * per_band, subs * NPIX), bf16),
            pltpu.VMEM((bands, 2 * steps * per_band, subs * NPIX), bf16),
            dma, dma, dma, dma,
        ],
        compiler_params=pltpu.CompilerParams(
            collective_id=0, has_side_effects=True, vmem_limit_bytes=VMEM_LIMIT
        ),
    )(owner, uv_coords, visibilities, aterms, lanes_dft, select)
    rows = TILE // bands
    scale = 1.0 / (NPIX * math.sqrt(width * chans * bands))
    return pl.pallas_call(
        functools.partial(place_kernel, (steps, subs, rows, TILE), scale),
        out_shape=jax.ShapeDtypeStruct((1, 2, rows, TILE), f32),
        in_specs=[hbm] * 4,
        out_specs=pl.BlockSpec(memory_space=pl.ANY),
        scratch_shapes=[
            pltpu.SMEM(offsets.shape, jnp.int32),
            pltpu.SMEM(counts.shape, jnp.int32),
            pltpu.VMEM(half.shape, f32),
            pltpu.VMEM(rows_dft.shape, f32),
            pltpu.VMEM((2 * NPIX, subs * NPIX), f32),
            pltpu.VMEM((2, rows + 2 * NPIX, TILE), f32),
            pltpu.SemaphoreType.DMA((4,)),
            dma,
        ],
        compiler_params=pltpu.CompilerParams(vmem_limit_bytes=VMEM_LIMIT),
    )(offsets, counts, half, rows_dft)


def solution(mesh):
    placed = (
        P("facet", None, "band", None, None),
        P(),
        P("facet", None, None, None, None),
        P("facet", None, None, None),
        P("facet", None),
        P(),
    )
    return jax.shard_map(
        body, mesh=mesh, in_specs=placed, out_specs=P("facet", None, "band", None), check_vma=False
    )
```

```python
import functools
import math

import jax
import jax.numpy as jnp
import numpy as np
from jax import lax
from jax.experimental import pallas as pl
from jax.experimental.pallas import tpu as pltpu
from jax.sharding import PartitionSpec as P

NPIX = 32
TILE = 2048
TWO_PI = 2.0 * math.pi
MESH = pl.DeviceIdType.MESH
HIGHEST = lax.Precision.HIGHEST
VMEM_LIMIT = 60 * 1024 * 1024
ROWS = 64


def cmul(a, b):
    return a[0] * b[0] - a[1] * b[1], a[0] * b[1] + a[1] * b[0]


def cheb(two_cos, now, before):
    return two_cos * now[0] - before[0], two_cos * now[1] - before[1]


def pick(mask, a, b):
    return jnp.where(mask, a[0], b[0]), jnp.where(mask, a[1], b[1])


def image_kernel(
    sizes, owner_hbm, uv_hbm, vis_hbm, ate_hbm, dft_hbm, sel_hbm, out_ref,
    owner_ref, uv_ref, vis_ref, ate_ref, dft_ref, sel_ref, load_sem,
    pow_ref, left_ref, right_ref, part_ref, cast_ref, got_ref, sum_ref, fac_ref, gain_ref,
    send_ref, band_ref, send_sem, recv_sem, send2_sem, recv2_sem, send3_sem, recv3_sem,
):
    facets, bands, steps, subs, chans, width = sizes
    per_band = NPIX // bands
    lanes = per_band * NPIX
    groups, stride = 4 // per_band, bands // facets
    fac, band = lax.axis_index("facet"), lax.axis_index("band")

    def in_band(k):
        return fac, lax.rem(band + k, bands)

    def in_facet(k):
        return lax.rem(fac + k, facets), band

    first = band * lanes // 128
    chunk = pl.ds(pl.multiple_of(first * 128, 128), 128)
    loads = [
        pltpu.make_async_copy(src, dst, load_sem.at[i])
        for i, (src, dst) in enumerate((
            (owner_hbm, owner_ref), (uv_hbm, uv_ref), (vis_hbm.at[0], vis_ref),
            (ate_hbm.at[0, :, :, :, chunk], ate_ref), (dft_hbm, dft_ref), (sel_hbm, sel_ref),
        ))
    ]
    for load in loads:
        load.start()
    barrier = pltpu.get_barrier_semaphore()

    for k in range(1, facets):
        pl.semaphore_signal(barrier, inc=1, device_id=in_facet(k), device_id_type=MESH)
    for k in range(1, bands):
        pl.semaphore_signal(barrier, inc=1, device_id=in_band(k), device_id_type=MESH)

    for load in loads[:3]:
        load.wait()
    step = jnp.int32(0)
    for t in range(steps):
        step = jnp.where(owner_ref[t] == fac, t, step)
    chan = band * chans + lax.broadcasted_iota(jnp.int32, (chans, 1), 0)
    freq = 1.0 + 0.5 * chan.astype(jnp.float32) / (chans * bands)
    for s in range(subs):
        uv = uv_ref[step, s]
        rows = pl.ds(s * chans, chans)
        for axis in range(2):
            angle = (TWO_PI / NPIX) * (uv[axis : axis + 1, :] * freq)
            w1 = (jnp.cos(angle), jnp.sin(angle))
            w2 = cmul(w1, w1)
            w4 = cmul(w2, w2)
            w8 = cmul(w4, w4)
            if axis == 0:
                w16 = cmul(w8, w8)
                kept = (w1, w4, w8, w16, cmul(w8, w16), cmul(w16, w16))
            else:
                kept = (w1, w2, cmul(w1, w2), w4, w8)
            for i, w in enumerate(kept):
                pow_ref[12 * axis + 2 * i, rows, :] = w[0]
                pow_ref[12 * axis + 2 * i + 1, rows, :] = w[1]

    j = lax.broadcasted_iota(jnp.int32, (8, width), 0)
    bit0, bit1, bit2 = (j & 1) == 1, (j & 2) == 2, (j & 4) == 4
    one = (jnp.ones((8, width), jnp.float32), jnp.zeros((8, width), jnp.float32))

    def subgrid(s):
        for c in range(chans):
            row = pl.ds(s * chans + c, 1)

            def power(index):
                return tuple(
                    jnp.broadcast_to(pow_ref[2 * index + part, row, :], (8, width))
                    for part in range(2)
                )

            cols = pl.ds(c * width, width)
            w1, w4, w8, w16, w24, w32 = (power(i) for i in range(6))
            value = vis_ref[s, c].astype(jnp.float32)
            vis = (
                jnp.broadcast_to(value[0:1], (8, width)),
                jnp.broadcast_to(value[1:2], (8, width)),
            )
            e = pick(bit1, pick(bit0, w24, w16), pick(bit0, w8, one))
            e = cmul(e, pick(bit2, one, (w32[0], -w32[1])))
            lower = cmul(vis, e)
            upper = cmul(lower, w4)
            two_cos = 2.0 * w1[0]
            seq_u = [upper, cmul(upper, w1)]
            seq_l = [lower, cmul(lower, w1)]
            for i in range(2, 4):
                seq_u.append(cheb(two_cos, seq_u[i - 1], seq_u[i - 2]))
                seq_l.append(cheb(two_cos, seq_l[i - 1], seq_l[i - 2]))
            for i in range(4):
                for part in range(2):
                    left_ref[pl.ds(ROWS * part + 16 * i, 16), cols] = jnp.concatenate(
                        [seq_l[i][part], seq_u[i][part]], axis=0
                    ).astype(jnp.bfloat16)
            r1, r2, r3, r4, r8 = (power(6 + i) for i in range(5))
            e = pick(bit1, pick(bit0, r3, r2), pick(bit0, r1, one))
            m2 = cmul(e, pick(bit2, r4, one))
            m3 = cmul(m2, r8)
            two_cos = 2.0 * r8[0]
            m1 = cheb(two_cos, m2, m3)
            m0 = cheb(two_cos, m1, m2)
            for part in range(2):
                right_ref[pl.ds(NPIX * part, 16), cols] = jnp.concatenate(
                    [m0[part], m1[part]], axis=0
                ).astype(jnp.bfloat16)
                right_ref[pl.ds(NPIX * part + 16, 16), cols] = jnp.concatenate(
                    [m2[part], m3[part]], axis=0
                ).astype(jnp.bfloat16)
        prod = lax.dot_general(
            left_ref[...], right_ref[...], (((1,), (1,)), ((), ())),
            preferred_element_type=jnp.float32,
        )
        re = prod[:ROWS, :NPIX] - prod[ROWS:, NPIX:]
        im = prod[:ROWS, NPIX:] + prod[ROWS:, :NPIX]
        for part, image in enumerate((re, im)):
            for high in range(4 // per_band):
                for odd in range(2):
                    pieces = []
                    for i in range(per_band):
                        at = 16 * (high * per_band + i) + 8 * odd
                        pieces.append(image[at : at + 8])
                    piece = jnp.concatenate(pieces, axis=1)
                    start, hop = odd * groups + high, 2 * groups // stride
                    for j in range(8):
                        part_ref[start % stride, start // stride + hop * j, 2 * s + part, :] = (
                            piece[j]
                        )

    for s in range(subs):
        subgrid(s)

    for b in range(bands):
        at = stride // 2 + b
        block = part_ref[at % stride, pl.ds(at // stride, facets)]
        cast_ref[b] = block.reshape(facets * 2 * subs, lanes).astype(jnp.bfloat16)

    pl.semaphore_wait(barrier, facets + bands - 2)

    def send(src, dst, sems, to):
        pltpu.make_async_remote_copy(
            src_ref=src, dst_ref=dst, send_sem=sems[0], recv_sem=sems[1],
            device_id=to, device_id_type=MESH,
        ).start()

    for k in range(1, bands):
        to = in_band(k)
        send(cast_ref.at[to[1]], got_ref.at[k], (send_sem, recv_sem), to)
    got_ref[0] = cast_ref[band]

    for load in loads[3:]:
        load.wait()
    for t in range(steps):
        for s in range(subs):
            gain = ate_ref[t, s].astype(jnp.float32)
            if lanes < 128:
                shift = lax.rem(band * lanes, 128)
                gain = sum(
                    jnp.where(shift == at, gain[:, at : at + lanes], 0.0)
                    for at in range(0, 128, lanes)
                )
            gain_ref[pl.ds(8 * t + 2 * s, 2), :] = gain

    def wait_all(buf, count, sem):
        view = buf.at[pl.ds(1, count)]
        pltpu.make_async_copy(view, view, sem).wait()

    wait_all(got_ref, bands - 1, recv_sem)
    acc = got_ref[0].astype(jnp.float32)
    for k in range(1, bands):
        acc = acc + got_ref[k].astype(jnp.float32)
    sum_ref[...] = acc.reshape(sum_ref.shape)
    for k in range(1, facets):
        to = in_facet(k)
        send(sum_ref.at[to[0]], fac_ref.at[k], (send2_sem, recv2_sem), to)
    fac_ref[0] = sum_ref[fac]
    wait_all(fac_ref, facets - 1, recv2_sem)
    image = jnp.concatenate(
        [fac_ref[lax.rem(fac + facets - owner_ref[t], facets)] for t in range(steps)], axis=0
    )
    gains = gain_ref[...]
    count = 8 * steps
    even = lax.broadcasted_iota(jnp.int32, (count, lanes), 0) % 2 == 0

    def nxt(x):
        return jnp.concatenate([x[1:], x[:1]], axis=0)

    def prev(x):
        return jnp.concatenate([x[-1:], x[:-1]], axis=0)

    straight = image * gains
    crossed = image * jnp.where(even, nxt(gains), prev(gains))
    weighted = jnp.where(even, straight - nxt(straight), crossed + prev(crossed))
    turned = jnp.where(even, nxt(weighted), -prev(weighted))
    both = jnp.concatenate([weighted, turned], axis=1)
    pixel = lax.broadcasted_iota(jnp.int32, both.shape, 1) % lanes // NPIX
    stacked = jnp.concatenate([jnp.where(pixel == i, both, 0.0) for i in range(per_band)], axis=0)
    half = jnp.dot(stacked, dft_ref[...], precision=HIGHEST, preferred_element_type=jnp.float32)
    row_sub = lax.broadcasted_iota(jnp.int32, half.shape, 0) % 8 // 2
    lane_sub = lax.broadcasted_iota(jnp.int32, half.shape, 1) // NPIX
    half = jnp.where(row_sub == lane_sub, half, 0.0)
    half = jnp.dot(sel_ref[...], half, precision=HIGHEST, preferred_element_type=jnp.float32)
    send_ref[...] = half.astype(jnp.bfloat16)

    for k in range(1, bands):
        send(send_ref, band_ref.at[k], (send3_sem, recv3_sem), in_band(k))
    band_ref[0] = send_ref[...]
    wait_all(band_ref, bands - 1, recv3_sem)
    group = 2 * per_band
    for b in range(bands):
        block = band_ref[lax.rem(band - b + bands, bands)].astype(jnp.float32)
        for t in range(steps):
            out_ref[t, pl.ds(group * b, group), :] = block[group * t : group * t + group]
    wait_all(got_ref, bands - 1, send_sem)
    wait_all(fac_ref, facets - 1, send2_sem)
    wait_all(band_ref, bands - 1, send3_sem)


def place_kernel(
    sizes, scale, off_hbm, cnt_hbm, half_hbm, dft_hbm, out_ref,
    off_ref, cnt_ref, half_ref, dft_ref, grid_ref, tile_ref, load_sem, sem,
):
    steps, subs, rows, cols = sizes
    loads = [
        pltpu.make_async_copy(src, dst, load_sem.at[i])
        for i, (src, dst) in enumerate((
            (off_hbm, off_ref), (cnt_hbm, cnt_ref), (half_hbm, half_ref), (dft_hbm, dft_ref),
        ))
    ]
    for load in loads:
        load.start()
    base = lax.axis_index("band") * rows
    tile_ref[:, pl.ds(NPIX, rows), :] = jnp.zeros((2, rows, cols), jnp.float32)
    lane = lax.broadcasted_iota(jnp.int32, (2 * NPIX, 128), 1)
    for load in loads:
        load.wait()

    def one_step(t, carry):
        grid_ref[...] = scale * jnp.dot(
            dft_ref[...], half_ref[t], precision=HIGHEST, preferred_element_type=jnp.float32
        )
        for s in range(subs):
            row = off_ref[0, t, 0, s] - base
            col = off_ref[0, t, 1, s]
            live = (s < cnt_ref[0, t]) & (row > -NPIX) & (row < rows)

            @pl.when(live)
            def _():
                shift = col % 128
                left = pl.multiple_of(col - shift, 128)
                grid = jnp.where(lane // NPIX == s, grid_ref[...], 0.0)
                grid = pltpu.roll(grid, (shift + 128 - NPIX * s) % 128, 1)
                down = (row + NPIX) % 8
                top = pl.multiple_of(row + NPIX - down, 8)
                tail = jnp.zeros((8, 128), jnp.float32)
                parts = [
                    pltpu.roll(
                        jnp.concatenate([grid[NPIX * part : NPIX * part + NPIX], tail], axis=0),
                        down, 0,
                    )
                    for part in range(2)
                ]
                span = lane[: NPIX + 8]
                for part in range(2):
                    spot = (part, pl.ds(top, NPIX + 8), pl.ds(left, 128))
                    tile_ref[spot] += jnp.where(span >= shift, parts[part], 0.0)

                @pl.when(shift > 128 - NPIX)
                def _():
                    right = pl.multiple_of(left + 128, 128)
                    for part in range(2):
                        spot = (part, pl.ds(top, NPIX + 8), pl.ds(right, 128))
                        tile_ref[spot] += jnp.where(span < shift, parts[part], 0.0)

        return carry

    lax.fori_loop(0, steps, one_step, 0)
    copy = pltpu.make_async_copy(tile_ref.at[:, pl.ds(NPIX, rows), :], out_ref.at[0], sem)
    copy.start()
    copy.wait()


def tables(bands, steps, subs):
    per_band = NPIX // bands
    k = np.arange(NPIX)
    angle = 2.0 * np.pi * (k[:, None] * k[None, :] % NPIX) / NPIX
    cos, sin = np.cos(angle), np.sin(angle)
    lanes_dft = np.concatenate(
        [np.tile(cos, (per_band, subs)), np.tile(sin, (per_band, subs))], axis=0
    )
    select = np.zeros((steps, 2, per_band, per_band, steps, subs, 2))
    for t in range(steps):
        for part in range(2):
            for i in range(per_band):
                select[t, part, i, i, t, :, part] = 1.0
    select = select.reshape(steps * 2 * per_band, per_band * steps * subs * 2)
    blocks = np.stack([np.stack([cos, sin]), np.stack([-sin, cos])])
    rows_dft = blocks.reshape(2, 2, NPIX, bands, per_band).transpose(0, 2, 3, 1, 4)
    rows_dft = rows_dft.reshape(2 * NPIX, 2 * NPIX)
    return [np.asarray(x, np.float32) for x in (lanes_dft, select, rows_dft)]


def body(visibilities, uv_coords, aterms, offsets, counts, owner):
    facets, bands = lax.axis_size("facet"), lax.axis_size("band")
    subs, chans, width = visibilities.shape[1], visibilities.shape[2], visibilities.shape[4]
    steps = owner.shape[0]
    per_band = NPIX // bands
    lanes, stride = per_band * NPIX, bands // facets
    lanes_dft, select, rows_dft = tables(bands, steps, subs)
    vmem = pl.BlockSpec(memory_space=pltpu.VMEM)
    hbm = pl.BlockSpec(memory_space=pltpu.HBM)
    f32, bf16 = jnp.float32, jnp.bfloat16
    dma = pltpu.SemaphoreType.DMA(())
    half = pl.pallas_call(
        functools.partial(image_kernel, (facets, bands, steps, subs, chans, width)),
        out_shape=jax.ShapeDtypeStruct((steps, 2 * NPIX, subs * NPIX), f32),
        in_specs=[hbm] * 6,
        out_specs=vmem,
        scratch_shapes=[
            pltpu.SMEM(owner.shape, jnp.int32),
            pltpu.VMEM(uv_coords.shape, f32),
            pltpu.VMEM(visibilities.shape[1:], bf16),
            pltpu.VMEM((steps, subs, 2, 128), bf16),
            pltpu.VMEM(lanes_dft.shape, f32),
            pltpu.VMEM(select.shape, f32),
            pltpu.SemaphoreType.DMA((6,)),
            pltpu.VMEM((22, subs * chans, width), f32),
            pltpu.VMEM((2 * ROWS, chans * width), bf16),
            pltpu.VMEM((2 * NPIX, chans * width), bf16),
            pltpu.VMEM((stride, ROWS // per_band // stride, 2 * subs, lanes), f32),
            pltpu.VMEM((bands, facets * 2 * subs, lanes), bf16),
            pltpu.VMEM((bands, facets * 2 * subs, lanes), bf16),
            pltpu.VMEM((facets, 2 * subs, lanes), f32),
            pltpu.VMEM((facets, 2 * subs, lanes), f32),
            pltpu.VMEM((8 * steps, lanes), f32),
            pltpu.VMEM((2 * steps * per_band, subs * NPIX), bf16),
            pltpu.VMEM((bands, 2 * steps * per_band, subs * NPIX), bf16),
            dma, dma, dma, dma, dma, dma,
        ],
        compiler_params=pltpu.CompilerParams(
            collective_id=0, has_side_effects=True, vmem_limit_bytes=VMEM_LIMIT
        ),
    )(owner, uv_coords, visibilities, aterms, lanes_dft, select)
    rows = TILE // bands
    scale = 1.0 / (NPIX * math.sqrt(width * chans * bands))
    return pl.pallas_call(
        functools.partial(place_kernel, (steps, subs, rows, TILE), scale),
        out_shape=jax.ShapeDtypeStruct((1, 2, rows, TILE), f32),
        in_specs=[hbm] * 4,
        out_specs=pl.BlockSpec(memory_space=pl.ANY),
        scratch_shapes=[
            pltpu.SMEM(offsets.shape, jnp.int32),
            pltpu.SMEM(counts.shape, jnp.int32),
            pltpu.VMEM(half.shape, f32),
            pltpu.VMEM(rows_dft.shape, f32),
            pltpu.VMEM((2 * NPIX, subs * NPIX), f32),
            pltpu.VMEM((2, rows + 2 * NPIX, TILE), f32),
            pltpu.SemaphoreType.DMA((4,)),
            dma,
        ],
        compiler_params=pltpu.CompilerParams(vmem_limit_bytes=VMEM_LIMIT),
    )(offsets, counts, half, rows_dft)


def solution(mesh):
    placed = (
        P("facet", None, "band", None, None),
        P(),
        P("facet", None, None, None, None),
        P("facet", None, None, None),
        P("facet", None),
        P(),
    )
    return jax.shard_map(
        body, mesh=mesh, in_specs=placed, out_specs=P("facet", None, "band", None), check_vma=False
    )
```

```python
import functools
import math

import jax
import jax.numpy as jnp
import numpy as np
from jax import lax
from jax.experimental import pallas as pl
from jax.experimental.pallas import tpu as pltpu
from jax.sharding import PartitionSpec as P

NPIX = 32
TILE = 2048
TWO_PI = 2.0 * math.pi
MESH = pl.DeviceIdType.MESH
HIGHEST = lax.Precision.HIGHEST
VMEM_LIMIT = 60 * 1024 * 1024
ROWS = 64


def cmul(a, b):
    return a[0] * b[0] - a[1] * b[1], a[0] * b[1] + a[1] * b[0]


def cheb(two_cos, now, before):
    return two_cos * now[0] - before[0], two_cos * now[1] - before[1]


def pick(mask, a, b):
    return jnp.where(mask, a[0], b[0]), jnp.where(mask, a[1], b[1])


def image_kernel(
    sizes, owner_hbm, uv_hbm, vis_hbm, ate_hbm, dft_hbm, sel_hbm, out_ref,
    owner_ref, uv_ref, vis_ref, ate_ref, dft_ref, sel_ref, load_sem,
    pow_ref, left_ref, right_ref, part_ref, got_ref, sum_ref, gain_ref, send_ref, band_ref,
    send_sem, recv_sem, send2_sem, recv2_sem,
):
    facets, bands, steps, subs, chans, width = sizes
    per_band = NPIX // bands
    lanes = per_band * NPIX
    total = facets * bands
    fac, band = lax.axis_index("facet"), lax.axis_index("band")
    me = fac * bands + band

    first = band * lanes // 128
    chunk = pl.ds(pl.multiple_of(first * 128, 128), 128)
    loads = [
        pltpu.make_async_copy(src, dst, load_sem.at[i])
        for i, (src, dst) in enumerate((
            (owner_hbm, owner_ref), (uv_hbm, uv_ref), (vis_hbm.at[0], vis_ref),
            (ate_hbm.at[0, :, :, :, chunk], ate_ref), (dft_hbm, dft_ref), (sel_hbm, sel_ref),
        ))
    ]
    for load in loads:
        load.start()
    barrier = pltpu.get_barrier_semaphore()

    def greet(k, carry):
        to = lax.rem(me + k, total)
        pl.semaphore_signal(
            barrier, inc=1, device_id=(to // bands, lax.rem(to, bands)), device_id_type=MESH
        )
        return carry

    lax.fori_loop(1, total, greet, 0)

    for load in loads[:3]:
        load.wait()
    step = jnp.int32(0)
    for t in range(steps):
        step = jnp.where(owner_ref[t] == fac, t, step)
    chan = band * chans + lax.broadcasted_iota(jnp.int32, (chans, 1), 0)
    freq = 1.0 + 0.5 * chan.astype(jnp.float32) / (chans * bands)
    for s in range(subs):
        uv = uv_ref[step, s]
        rows = pl.ds(s * chans, chans)
        for axis in range(2):
            angle = (TWO_PI / NPIX) * (uv[axis : axis + 1, :] * freq)
            w1 = (jnp.cos(angle), jnp.sin(angle))
            w2 = cmul(w1, w1)
            w4 = cmul(w2, w2)
            w8 = cmul(w4, w4)
            if axis == 0:
                w16 = cmul(w8, w8)
                kept = (w1, w4, w8, cmul(w4, w8), w16, cmul(w16, w16))
            else:
                kept = (w1, w2, cmul(w1, w2), w4, w8)
            for i, w in enumerate(kept):
                pow_ref[12 * axis + 2 * i, rows, :] = w[0]
                pow_ref[12 * axis + 2 * i + 1, rows, :] = w[1]

    j = lax.broadcasted_iota(jnp.int32, (8, width), 0)
    bit0, bit1, bit2 = (j & 1) == 1, (j & 2) == 2, (j & 4) == 4
    one = (jnp.ones((8, width), jnp.float32), jnp.zeros((8, width), jnp.float32))

    def subgrid(s):
        for c in range(chans):
            row = pl.ds(s * chans + c, 1)

            def power(index):
                return tuple(
                    jnp.broadcast_to(pow_ref[2 * index + part, row, :], (8, width))
                    for part in range(2)
                )

            cols = pl.ds(c * width, width)
            w1, w4, w8, w12, w16, w32 = (power(i) for i in range(6))
            value = vis_ref[s, c].astype(jnp.float32)
            vis = (
                jnp.broadcast_to(value[0:1], (8, width)),
                jnp.broadcast_to(value[1:2], (8, width)),
            )
            e = pick(bit1, pick(bit0, w12, w8), pick(bit0, w4, one))
            e = cmul(e, pick(bit2, w16, one))
            upper = cmul(vis, e)
            lower = cmul(upper, (w32[0], -w32[1]))
            two_cos = 2.0 * w1[0]
            seq_u = [upper, cmul(upper, w1)]
            seq_l = [lower, cmul(lower, w1)]
            for i in range(2, 4):
                seq_u.append(cheb(two_cos, seq_u[i - 1], seq_u[i - 2]))
                seq_l.append(cheb(two_cos, seq_l[i - 1], seq_l[i - 2]))
            for i in range(4):
                for part in range(2):
                    left_ref[pl.ds(ROWS * part + 16 * i, 16), cols] = jnp.concatenate(
                        [seq_l[i][part], seq_u[i][part]], axis=0
                    ).astype(jnp.bfloat16)
            r1, r2, r3, r4, r8 = (power(6 + i) for i in range(5))
            e = pick(bit1, pick(bit0, r3, r2), pick(bit0, r1, one))
            m2 = cmul(e, pick(bit2, r4, one))
            m3 = cmul(m2, r8)
            two_cos = 2.0 * r8[0]
            m1 = cheb(two_cos, m2, m3)
            m0 = cheb(two_cos, m1, m2)
            for part in range(2):
                right_ref[pl.ds(NPIX * part, 16), cols] = jnp.concatenate(
                    [m0[part], m1[part]], axis=0
                ).astype(jnp.bfloat16)
                right_ref[pl.ds(NPIX * part + 16, 16), cols] = jnp.concatenate(
                    [m2[part], m3[part]], axis=0
                ).astype(jnp.bfloat16)
        prod = lax.dot_general(
            left_ref[...], right_ref[...], (((1,), (1,)), ((), ())),
            preferred_element_type=jnp.float32,
        )
        re = prod[:ROWS, :NPIX] - prod[ROWS:, NPIX:]
        im = prod[:ROWS, NPIX:] + prod[ROWS:, :NPIX]
        for part, image in enumerate((re, im)):
            for high in range(4 // per_band):
                pieces = [
                    image[16 * (high * per_band + i) : 16 * (high * per_band + i) + 16]
                    for i in range(per_band)
                ]
                part_ref[:, high, 2 * s + part, :] = jnp.concatenate(pieces, axis=1)

    for s in range(subs):
        subgrid(s)

    pl.semaphore_wait(barrier, total - 1)

    groups = 4 // per_band

    def source(to):
        at = (to // bands * (NPIX // facets) + NPIX // 2 // facets) // per_band + lax.rem(to, bands)
        return part_ref.at[at // groups, lax.rem(at, groups)]

    def spread(k, carry):
        to = lax.rem(me + k, total)
        pltpu.make_async_remote_copy(
            src_ref=source(to), dst_ref=got_ref.at[k], send_sem=send_sem, recv_sem=recv_sem,
            device_id=(to // bands, lax.rem(to, bands)), device_id_type=MESH,
        ).start()
        return carry

    lax.fori_loop(1, total, spread, 0)
    got_ref[0] = source(me)[...]

    for load in loads[3:]:
        load.wait()
    for t in range(steps):
        for s in range(subs):
            gain = ate_ref[t, s].astype(jnp.float32)
            if lanes < 128:
                shift = lax.rem(band * lanes, 128)
                gain = sum(
                    jnp.where(shift == at, gain[:, at : at + lanes], 0.0)
                    for at in range(0, 128, lanes)
                )
            gain_ref[pl.ds(8 * t + 2 * s, 2), :] = gain

    def wait_all(buf, count, sem):
        view = buf.at[pl.ds(1, count)]
        pltpu.make_async_copy(view, view, sem).wait()

    wait_all(got_ref, total - 1, recv_sem)
    for g in range(facets):
        acc = got_ref[lax.rem(me - g * bands + total, total)]
        for b in range(1, bands):
            acc = acc + got_ref[lax.rem(me - g * bands - b + 2 * total, total)]
        sum_ref[g] = acc
    image = jnp.concatenate([sum_ref[owner_ref[t]] for t in range(steps)], axis=0)
    gains = gain_ref[...]
    count = 8 * steps
    even = lax.broadcasted_iota(jnp.int32, (count, lanes), 0) % 2 == 0

    def nxt(x):
        return jnp.concatenate([x[1:], x[:1]], axis=0)

    def prev(x):
        return jnp.concatenate([x[-1:], x[:-1]], axis=0)

    straight = image * gains
    crossed = image * jnp.where(even, nxt(gains), prev(gains))
    weighted = jnp.where(even, straight - nxt(straight), crossed + prev(crossed))
    turned = jnp.where(even, nxt(weighted), -prev(weighted))
    both = jnp.concatenate([weighted, turned], axis=1)
    pixel = lax.broadcasted_iota(jnp.int32, both.shape, 1) % lanes // NPIX
    stacked = jnp.concatenate([jnp.where(pixel == i, both, 0.0) for i in range(per_band)], axis=0)
    half = jnp.dot(stacked, dft_ref[...], precision=HIGHEST, preferred_element_type=jnp.float32)
    row_sub = lax.broadcasted_iota(jnp.int32, half.shape, 0) % 8 // 2
    lane_sub = lax.broadcasted_iota(jnp.int32, half.shape, 1) // NPIX
    half = jnp.where(row_sub == lane_sub, half, 0.0)
    half = jnp.dot(
        sel_ref[...].astype(jnp.bfloat16), half.astype(jnp.bfloat16),
        preferred_element_type=jnp.float32,
    )
    send_ref[...] = half.astype(jnp.bfloat16)

    def share(k, carry):
        pltpu.make_async_remote_copy(
            src_ref=send_ref, dst_ref=band_ref.at[k], send_sem=send2_sem, recv_sem=recv2_sem,
            device_id=(fac, lax.rem(band + k, bands)), device_id_type=MESH,
        ).start()
        return carry

    lax.fori_loop(1, bands, share, 0)
    band_ref[0] = send_ref[...]
    wait_all(band_ref, bands - 1, recv2_sem)
    group = 2 * per_band
    for b in range(bands):
        block = band_ref[lax.rem(band - b + bands, bands)].astype(jnp.float32)
        for t in range(steps):
            out_ref[t, pl.ds(group * b, group), :] = block[group * t : group * t + group]
    wait_all(got_ref, total - 1, send_sem)
    wait_all(band_ref, bands - 1, send2_sem)


def place_kernel(
    sizes, scale, off_hbm, cnt_hbm, half_hbm, dft_hbm, out_ref,
    off_ref, cnt_ref, half_ref, dft_ref, grid_ref, tile_ref, load_sem, sem,
):
    steps, subs, rows, cols = sizes
    loads = [
        pltpu.make_async_copy(src, dst, load_sem.at[i])
        for i, (src, dst) in enumerate((
            (off_hbm, off_ref), (cnt_hbm, cnt_ref), (half_hbm, half_ref), (dft_hbm, dft_ref),
        ))
    ]
    for load in loads:
        load.start()
    base = lax.axis_index("band") * rows
    split = rows // 2
    cuts = (NPIX, min(split + 2 * NPIX, rows + NPIX), rows + NPIX)

    def clear(first, last):
        if last > first:
            tile_ref[:, pl.ds(first, last - first), :] = jnp.zeros(
                (2, last - first, cols), jnp.float32
            )

    def write(at):
        return pltpu.make_async_copy(
            tile_ref.at[:, pl.ds(NPIX + at * split, split), :],
            out_ref.at[0, :, pl.ds(at * split, split), :], sem.at[at],
        )

    clear(cuts[0], cuts[1])
    lane = lax.broadcasted_iota(jnp.int32, (2 * NPIX, 128), 1)
    for load in loads:
        load.wait()

    table = dft_ref[...]
    high = table.astype(jnp.bfloat16)
    low = (table - high.astype(jnp.float32)).astype(jnp.bfloat16)
    table = jnp.concatenate([high, low], axis=0)
    for t in range(steps):
        both = jnp.dot(
            table, half_ref[t].astype(jnp.bfloat16), preferred_element_type=jnp.float32
        )
        grid_ref[t] = scale * (both[: 2 * NPIX] + both[2 * NPIX :])

    def one_step(at, t, carry):
        for s in range(subs):
            row = off_ref[0, t, 0, s] - base
            col = off_ref[0, t, 1, s]
            live = (s < cnt_ref[0, t]) & (row < rows)
            live = live & ((row > -NPIX) & (row < split) if at == 0 else row >= split)

            @pl.when(live)
            def _():
                shift = col % 128
                left = pl.multiple_of(col - shift, 128)
                grid = jnp.where(lane // NPIX == s, grid_ref[t], 0.0)
                grid = pltpu.roll(grid, (shift + 128 - NPIX * s) % 128, 1)
                down = (row + NPIX) % 8
                top = pl.multiple_of(row + NPIX - down, 8)
                tail = jnp.zeros((8, 128), jnp.float32)
                parts = [
                    pltpu.roll(
                        jnp.concatenate([grid[NPIX * part : NPIX * part + NPIX], tail], axis=0),
                        down, 0,
                    )
                    for part in range(2)
                ]
                span = lane[: NPIX + 8]
                for part in range(2):
                    spot = (part, pl.ds(top, NPIX + 8), pl.ds(left, 128))
                    tile_ref[spot] += jnp.where(span >= shift, parts[part], 0.0)

                @pl.when(shift > 128 - NPIX)
                def _():
                    right = pl.multiple_of(left + 128, 128)
                    for part in range(2):
                        spot = (part, pl.ds(top, NPIX + 8), pl.ds(right, 128))
                        tile_ref[spot] += jnp.where(span < shift, parts[part], 0.0)

        return carry

    lax.fori_loop(0, steps, functools.partial(one_step, 0), 0)
    write(0).start()
    clear(cuts[1], cuts[2])
    lax.fori_loop(0, steps, functools.partial(one_step, 1), 0)
    write(1).start()
    write(0).wait()
    write(1).wait()


def tables(bands, steps, subs):
    per_band = NPIX // bands
    k = np.arange(NPIX)
    angle = 2.0 * np.pi * (k[:, None] * k[None, :] % NPIX) / NPIX
    cos, sin = np.cos(angle), np.sin(angle)
    lanes_dft = np.concatenate(
        [np.tile(cos, (per_band, subs)), np.tile(sin, (per_band, subs))], axis=0
    )
    select = np.zeros((steps, 2, per_band, per_band, steps, subs, 2))
    for t in range(steps):
        for part in range(2):
            for i in range(per_band):
                select[t, part, i, i, t, :, part] = 1.0
    select = select.reshape(steps * 2 * per_band, per_band * steps * subs * 2)
    blocks = np.stack([np.stack([cos, sin]), np.stack([-sin, cos])])
    rows_dft = blocks.reshape(2, 2, NPIX, bands, per_band).transpose(0, 2, 3, 1, 4)
    rows_dft = rows_dft.reshape(2 * NPIX, 2 * NPIX)
    return [np.asarray(x, np.float32) for x in (lanes_dft, select, rows_dft)]


def body(visibilities, uv_coords, aterms, offsets, counts, owner):
    facets, bands = lax.axis_size("facet"), lax.axis_size("band")
    subs, chans, width = visibilities.shape[1], visibilities.shape[2], visibilities.shape[4]
    steps = owner.shape[0]
    per_band = NPIX // bands
    lanes = per_band * NPIX
    total = facets * bands
    lanes_dft, select, rows_dft = tables(bands, steps, subs)
    vmem = pl.BlockSpec(memory_space=pltpu.VMEM)
    hbm = pl.BlockSpec(memory_space=pltpu.HBM)
    f32, bf16 = jnp.float32, jnp.bfloat16
    dma = pltpu.SemaphoreType.DMA(())
    half = pl.pallas_call(
        functools.partial(image_kernel, (facets, bands, steps, subs, chans, width)),
        out_shape=jax.ShapeDtypeStruct((steps, 2 * NPIX, subs * NPIX), f32),
        in_specs=[hbm] * 6,
        out_specs=vmem,
        scratch_shapes=[
            pltpu.SMEM(owner.shape, jnp.int32),
            pltpu.VMEM(uv_coords.shape, f32),
            pltpu.VMEM(visibilities.shape[1:], bf16),
            pltpu.VMEM((steps, subs, 2, 128), bf16),
            pltpu.VMEM(lanes_dft.shape, f32),
            pltpu.VMEM(select.shape, f32),
            pltpu.SemaphoreType.DMA((6,)),
            pltpu.VMEM((22, subs * chans, width), f32),
            pltpu.VMEM((2 * ROWS, chans * width), bf16),
            pltpu.VMEM((2 * NPIX, chans * width), bf16),
            pltpu.VMEM((16, 4 // per_band, 2 * subs, lanes), f32),
            pltpu.VMEM((total, 2 * subs, lanes), f32),
            pltpu.VMEM((facets, 2 * subs, lanes), f32),
            pltpu.VMEM((8 * steps, lanes), f32),
            pltpu.VMEM((2 * steps * per_band, subs * NPIX), bf16),
            pltpu.VMEM((bands, 2 * steps * per_band, subs * NPIX), bf16),
            dma, dma, dma, dma,
        ],
        compiler_params=pltpu.CompilerParams(
            collective_id=0, has_side_effects=True, vmem_limit_bytes=VMEM_LIMIT
        ),
    )(owner, uv_coords, visibilities, aterms, lanes_dft, select)
    rows = TILE // bands
    scale = 1.0 / (NPIX * math.sqrt(width * chans * bands))
    return pl.pallas_call(
        functools.partial(place_kernel, (steps, subs, rows, TILE), scale),
        out_shape=jax.ShapeDtypeStruct((1, 2, rows, TILE), f32),
        in_specs=[hbm] * 4,
        out_specs=pl.BlockSpec(memory_space=pl.ANY),
        scratch_shapes=[
            pltpu.SMEM(offsets.shape, jnp.int32),
            pltpu.SMEM(counts.shape, jnp.int32),
            pltpu.VMEM(half.shape, f32),
            pltpu.VMEM(rows_dft.shape, f32),
            pltpu.VMEM((steps, 2 * NPIX, subs * NPIX), f32),
            pltpu.VMEM((2, rows + 2 * NPIX, TILE), f32),
            pltpu.SemaphoreType.DMA((4,)),
            pltpu.SemaphoreType.DMA((2,)),
        ],
        compiler_params=pltpu.CompilerParams(vmem_limit_bytes=VMEM_LIMIT),
    )(offsets, counts, half, rows_dft)


def solution(mesh):
    placed = (
        P("facet", None, "band", None, None),
        P(),
        P("facet", None, None, None, None),
        P("facet", None, None, None),
        P("facet", None),
        P(),
    )
    return jax.shard_map(
        body, mesh=mesh, in_specs=placed, out_specs=P("facet", None, "band", None), check_vma=False
    )
```
